256 devices in a mesh: seq: 8 (over x_hi, y), ch: 32 (over x_lo, z, core).
Axes of the slice: x: 4 (x_hi: 2, x_lo: 2; x = x_hi * 2 + x_lo), y: 4, z: 8, core: 2. Of those that a mesh axis runs over, the one named last changes fastest.
Arguments:
- tokens: bfloat16 [8192, 4096], P('seq', 'ch'), may hold values from -400 to 400, as said below
- sign_bits: int32 [4096], replicated, may hold values from 0 to 1
- norm_gain: float32 [4096], replicated, may hold values from 0.1 to 1.9
- code_indices: int32 [4096, 3, 4096], P(None, None, 'ch'), may hold values from 0 to 3
- codebook: float32 [4], replicated, may hold values from -1.5 to 1.5
- col_scale: float32 [3, 4096], P(None, 'ch'), may hold values from 0.008 to 0.03
- group_ids: int32 [4096], P('ch'), may hold values from 0 to 255
- filters: float32 [256, 128], replicated, may hold values from -0.5 to 0.5
- skip_gain: float32 [4096], P('ch'), may hold values from 0.5 to 1.5
- out_weight: bfloat16 [4096, 4096], P(None, 'ch'), may hold values from -0.09375 to 0.09375
Outputs:
- mixed: bfloat16 [8192, 4096], P('seq', 'ch')
The draws below stay inside these ranges and needn't reach their ends.
Inputs may be any that keep to these rules, and one draw needn't show every extreme that they name: `tokens`: each token row and each feature column carries its own positive scale.
All inputs are finite; a program needn't handle non-finite values.
Results may differ from the reference program's by a relative error of at most 0.01.
Values may be sent and summed in bfloat16 or wider, within the bound.
No kernel may reach another device: no remote copies, remote signals or barrier semaphores. Data moves between devices by JAX's collectives and lax.ppermute only.
A program may use at most 128 MiB of HBM per device.

```python
import math
import jax
import jax.numpy as jnp
from jax import lax

D = 4096
FLEN = 128
FILT = 256
LEVELS = 4
TOKENS = 8192


def draw_tokens(key, part):
    key_rows, key_cols, key_base = jax.random.split(key, 3)
    row_scale = jnp.exp(jax.random.uniform(key_rows, (TOKENS, 1), jnp.float32, 0.0, math.log(10.0)))
    col_scale = jnp.exp(jax.random.uniform(key_cols, (1, D), jnp.float32, 0.0, math.log(10.0)))
    base = jnp.clip(jax.random.normal(key_base, (TOKENS, D), jnp.float32), -4.0, 4.0)
    return (base * row_scale * col_scale).astype(jnp.bfloat16)


def plant(entries, own_key, smallest, top_value):
    extent = entries.shape
    place = [jax.random.randint(jax.random.fold_in(own_key, axis), (), 0, extent[axis]) for axis in range(len(extent))]
    entries = entries.at[tuple(place)].set(smallest)
    longest = extent.index(max(extent))
    place[longest] = (place[longest] + 1) % extent[longest]
    return entries.at[tuple(place)].set(top_value)


def steps_of(key, dims, pieces, smallest, high):
    level = 1.0
    for position, shards_of in pieces:
        draws = jax.random.uniform(jax.random.fold_in(jax.random.fold_in(key, 6), position), (shards_of,), jnp.float32, smallest / len(pieces), high / len(pieces))
        level = level * jnp.repeat(jnp.exp(draws), dims[position] // shards_of).reshape((-1,) + (1,) * (len(dims) - 1 - position))
    return level


def noise(key, extent, scale, reach, cuts=(), kind=jnp.bfloat16):
    drawn = scale * jax.random.normal(key, extent, jnp.float32)
    if cuts:
        drawn = drawn * steps_of(key, extent, cuts, -0.22, 0.18)
    return jnp.clip(drawn, -reach, reach).astype(kind)


def setup_inputs(seed: int = 0) -> dict:
    keys = jax.random.split(jax.random.key(seed), 11)
    return {
        "tokens": draw_tokens(jax.random.fold_in(keys[10], 71), 0),
        "sign_bits": plant(jax.random.randint(keys[1], (D,), 0, 2), jax.random.fold_in(keys[1], 1), 0, 1).astype(jnp.int32),
        "norm_gain": jnp.clip(1.0 + 0.18 * jax.random.normal(keys[2], (D,), jnp.float32), 0.1, 1.9),
        "code_indices": plant(jax.random.randint(keys[3], (D, 3, D), 0, 4), jax.random.fold_in(keys[3], 1), 0, 3).astype(jnp.int32),
        "codebook": jnp.clip(jax.random.uniform(keys[4], (LEVELS,), jnp.float32, -1.5, 1.5), -1.5, 1.5),
        "col_scale": jnp.clip(jnp.exp(math.log(0.03) - 1.3217558 * jax.random.uniform(keys[5], (3, D), jnp.float32) ** steps_of(keys[5], (3, D), ((1, 32),), -0.2, 0.2)), 0.008, 0.03),
        "group_ids": plant(jax.random.randint(keys[6], (D,), 0, FILT), jax.random.fold_in(keys[6], 1), 0, FILT - 1).astype(jnp.int32),
        "filters": noise(keys[7], (FILT, FLEN), FLEN ** -0.5, 0.5, (), jnp.float32),
        "skip_gain": jnp.clip(0.5 + 1.0 * jax.random.uniform(keys[8], (D,), jnp.float32) ** steps_of(keys[8], (D,), ((0, 32),), -0.2, 0.2), 0.5, 1.5),
        "out_weight": noise(keys[9], (D, D), D ** -0.5, 0.09375, ((1, 32),)),
    }


def hadamard(order):
    index_vec = jnp.arange(order, dtype=jnp.int32)
    anded = index_vec[:, None] & index_vec[None, :]
    parity = jnp.zeros((order, order), jnp.int32)
    for bit_pos in range(order.bit_length()):
        parity = parity + (anded >> bit_pos & 1)
    return (1 - 2 * (parity % 2)).astype(jnp.float32)

def rotate(floats):
    row_count = floats.shape[0]
    model_width = floats.shape[1]
    bit_count = model_width.bit_length() - 1
    outer_size = 2 ** ((bit_count + 1) // 2)
    inner_size = model_width // outer_size
    shaped = floats.reshape(row_count, outer_size, inner_size)
    shaped = jnp.einsum('tab,ac->tcb', shaped, hadamard(outer_size), precision=lax.Precision.HIGHEST)
    shaped = jnp.einsum('tcb,bd->tcd', shaped, hadamard(inner_size), precision=lax.Precision.HIGHEST)
    return shaped.reshape(row_count, model_width) / math.sqrt(model_width)

def reference(tokens, sign_bits, norm_gain, code_indices, codebook, col_scale, group_ids, filters, skip_gain, out_weight):
    floats = tokens.astype(jnp.float32)
    inverse = lax.rsqrt(lax.optimization_barrier(jnp.mean(floats * floats, axis=-1, keepdims=True)) + 1e-05)
    signed = (2 * sign_bits - 1).astype(jnp.float32)
    normed = floats * inverse * norm_gain * signed
    rotated = rotate(normed).astype(jnp.bfloat16)
    weights = (codebook[code_indices] * col_scale[None, :, :]).astype(jnp.bfloat16)
    projected = jnp.dot(rotated, weights.reshape(D, 3 * D), preferred_element_type=jnp.float32).reshape(TOKENS, 3, D)
    gate_side = projected[:, 0, :]
    key_side = projected[:, 1, :]
    value_side = projected[:, 2, :]
    product = (key_side * value_side).astype(jnp.bfloat16)
    product_f = product.astype(jnp.float32)
    channel_taps = filters[group_ids]
    padded = jnp.pad(product_f, ((FLEN - 1, 0), (0, 0)))
    filtered = jnp.zeros((TOKENS, D), jnp.float32)
    for lag_index in range(FLEN):
        begin = FLEN - 1 - lag_index
        filtered = filtered + padded[begin:begin + TOKENS] * channel_taps[:, lag_index][None, :]
    hidden = (gate_side * (filtered + skip_gain * product_f)).astype(jnp.bfloat16)
    return jnp.dot(hidden, out_weight, preferred_element_type=jnp.float32).astype(jnp.bfloat16)
```

```python
import functools

import jax
import jax.numpy as jnp
import numpy as np
from jax import lax
from jax.experimental import pallas as pl
from jax.experimental.pallas import tpu as pltpu
from jax.sharding import Mesh
from jax.sharding import PartitionSpec as P

BF = jnp.bfloat16
F32 = jnp.float32
MB = 1024 * 1024
SWAP = [(0, 1), (1, 0)]


def hadamard_np(order):
    index = np.arange(order)
    anded = index[:, None] & index[None, :]
    parity = np.zeros((order, order), np.int64)
    for bit in range(order.bit_length()):
        parity += anded >> bit & 1
    return (1 - 2 * (parity % 2)).astype(np.float32)


def dot(a, b):
    return jnp.dot(a, b, preferred_element_type=F32)


def weight_kernel(book_ref, codes_ref, scale_ref, rows_ref, had_ref, out_ref, y_ref):
    outer = y_ref.shape[0]
    inner = y_ref.shape[1]
    scale = scale_ref[...].reshape(1, 128)
    values = [(book_ref[k] * scale).astype(BF).astype(F32) for k in range(4)]
    had = had_ref[...]
    for a in range(outer):
        codes = codes_ref[0, pl.ds(a * inner, inner), :]
        low = jnp.where(codes == 0, values[0], values[1])
        high = jnp.where(codes == 2, values[2], values[3])
        levels = jnp.where(codes < 2, low, high).astype(BF)
        y_ref[a] = dot(had, levels)

    def mix(i, carry):
        at = pl.multiple_of(i * 16, 16)
        parts = [y_ref[a, pl.ds(at, 16), :] for a in range(outer)]
        span = 1
        while span < outer:
            new = list(parts)
            for a in range(outer):
                if a & span:
                    new[a] = parts[a ^ span] - parts[a]
                else:
                    new[a] = parts[a] + parts[a ^ span]
            parts = new
            span *= 2
        for a in range(outer):
            rows = pl.ds(a * inner + at, 16)
            out_ref[rows, :] = (parts[a] * rows_ref[rows, :]).astype(BF)
        return carry

    lax.fori_loop(0, inner // 16, mix, 0)


def make_weights(book, codes, scale, rows, had, branch):
    width = codes.shape[1]
    inner = had.shape[0]
    return pl.pallas_call(
        weight_kernel,
        grid=(1,),
        in_specs=[
            pl.BlockSpec(memory_space=pltpu.SMEM),
            pl.BlockSpec((1, width, 128), lambda i: (branch, 0, 0)),
            pl.BlockSpec((1, 1, 128), lambda i: (branch, 0, 0)),
            pl.BlockSpec((width, 128), lambda i: (0, 0)),
            pl.BlockSpec((inner, inner), lambda i: (0, 0)),
        ],
        out_specs=pl.BlockSpec((width, 128), lambda i: (0, 0)),
        out_shape=jax.ShapeDtypeStruct((width, 128), BF),
        scratch_shapes=[pltpu.VMEM((width // inner, inner, 128), F32)],
        compiler_params=pltpu.CompilerParams(vmem_limit_bytes=20 * MB),
        cost_estimate=pl.CostEstimate(
            flops=2 * width * inner * 128, bytes_accessed=width * 128 * 10, transcendentals=0
        ),
    )(book, codes, scale, rows, had)


def project_kernel(n, first, last, width, idx_ref, *refs):
    refs = list(refs)
    blocks = [refs.pop(0) for _ in range(n)]
    weights = [[[refs.pop(0) for _ in range(2)] for _ in range(3)] for _ in range(n)]
    if not first:
        acc_in = refs.pop(0)
        sq_in = refs.pop(0)
    rows = blocks[0].shape[0]
    out_refs = refs
    squares = None if first else sq_in[...]
    for k in range(n):
        wide = blocks[k][...].astype(F32)
        wide = wide * wide
        part = wide[:, :128] + wide[:, 128:]
        squares = part if squares is None else squares + part
    made = []
    for b in range(3):
        total = None if first else acc_in[:, b * 256 : (b + 1) * 256]
        for k in range(n):
            pair = jnp.concatenate([weights[k][b][0][...], weights[k][b][1][...]], axis=1)
            part = dot(blocks[k][...], pair)
            total = part if total is None else total + part
        if last:
            made.append(total)
        else:
            out_refs[0][:, b * 256 : (b + 1) * 256] = total
    if last:
        mean = jnp.sum(squares, axis=1, keepdims=True) / width
        inverse = lax.rsqrt(mean + 1e-05)
        out_refs[0][...] = made[0] * inverse
        out_refs[1][...] = ((made[1] * inverse) * (made[2] * inverse)).astype(BF)
    else:
        out_refs[1][...] = squares


def project(blocks, weights, index, state, last):
    n = len(blocks)
    rows = blocks[0].shape[0]
    width = weights[0][0].shape[0]
    first = state is None
    in_specs = [pl.BlockSpec((rows, 256), lambda i, idx: (0, 0)) for _ in range(n)]
    operands = list(blocks)
    for k in range(n):
        for b in range(3):
            for side in range(2):
                in_specs.append(pl.BlockSpec((256, 128), lambda i, idx, k=k: (idx[k], 0)))
                operands.append(weights[b][side])
    wide_spec = pl.BlockSpec((rows, 768), lambda i, idx: (0, 0))
    sq_spec = pl.BlockSpec((rows, 128), lambda i, idx: (0, 0))
    if not first:
        in_specs += [wide_spec, sq_spec]
        operands += list(state)
    if last:
        out_specs = [pl.BlockSpec((rows, 256), lambda i, idx: (0, 0))] * 2
        out_shape = [
            jax.ShapeDtypeStruct((rows, 256), F32),
            jax.ShapeDtypeStruct((rows, 256), BF),
        ]
    else:
        out_specs = [wide_spec, sq_spec]
        out_shape = [
            jax.ShapeDtypeStruct((rows, 768), F32),
            jax.ShapeDtypeStruct((rows, 128), F32),
        ]
    return pl.pallas_call(
        functools.partial(project_kernel, n, first, last, width),
        grid_spec=pltpu.PrefetchScalarGridSpec(
            num_scalar_prefetch=1, grid=(1,), in_specs=in_specs, out_specs=out_specs
        ),
        out_shape=out_shape,
        compiler_params=pltpu.CompilerParams(vmem_limit_bytes=32 * MB),
        cost_estimate=pl.CostEstimate(
            flops=2 * n * rows * 256 * 768, bytes_accessed=n * 655360 + 3 * MB, transcendentals=0
        ),
    )(index, *operands)


def filter_kernel(flag_ref, prev_ref, cur_ref, gate_ref, taps_a, taps_b, skip_a, skip_b, out_ref, s_ref):
    lead = prev_ref.shape[0]
    count = cur_ref.shape[0]
    ext = jnp.concatenate([prev_ref[...], cur_ref[...]], axis=0).astype(F32)
    s_ref[0] = ext
    for r in range(1, 8):
        s_ref[r] = pltpu.roll(ext, r, 0)

    def strip(i, carry):
        at = pl.multiple_of(i * 128, 128)
        made = []
        for side, (taps, skip) in enumerate(((taps_a, skip_a), (taps_b, skip_b))):
            lanes = slice(side * 128, side * 128 + 128)
            total = jnp.zeros((128, 128), F32)
            for r in range(8):
                for q in range(lead // 8):
                    j = 8 * q + r
                    moved = s_ref[r, pl.ds(pl.multiple_of(at + lead - 8 * q, 8), 128), lanes]
                    total = total + taps[j : j + 1, :] * moved
            own = s_ref[0, pl.ds(pl.multiple_of(at + lead, 8), 128), lanes]
            total = total + skip[...] * own
            made.append(gate_ref[pl.ds(at, 128), lanes] * total)
        here = flag_ref[0] == 0
        out_ref[pl.ds(at, 128), 0:128] = jnp.where(here, made[0], made[1]).astype(BF)
        out_ref[pl.ds(at, 128), 128:256] = jnp.where(here, made[1], made[0]).astype(BF)
        return carry

    lax.fori_loop(0, count // 128, strip, 0)


def filtered_part(flag, prev, prev_at, product, gate, part, taps, skips):
    lead = taps[0].shape[0]
    whole = lambda i, flag: (0, 0)
    return pl.pallas_call(
        filter_kernel,
        grid_spec=pltpu.PrefetchScalarGridSpec(
            num_scalar_prefetch=1,
            grid=(1,),
            in_specs=[
                pl.BlockSpec((lead, 256), lambda i, flag: (prev_at, 0)),
                pl.BlockSpec((256, 256), lambda i, flag: (part, 0)),
                pl.BlockSpec((256, 256), lambda i, flag: (part, 0)),
                pl.BlockSpec((lead, 128), whole),
                pl.BlockSpec((lead, 128), whole),
                pl.BlockSpec((1, 128), whole),
                pl.BlockSpec((1, 128), whole),
            ],
            out_specs=pl.BlockSpec((256, 256), whole),
            scratch_shapes=[pltpu.VMEM((8, lead + 256, 256), F32)],
        ),
        out_shape=jax.ShapeDtypeStruct((256, 256), BF),
        compiler_params=pltpu.CompilerParams(vmem_limit_bytes=16 * MB),
        cost_estimate=pl.CostEstimate(
            flops=2 * 128 * 256 * 256 * 32, bytes_accessed=MB, transcendentals=0
        ),
    )(flag, prev, product, gate, taps[0], taps[1], skips[0], skips[1])


def out_kernel(n, first, last, idx_ref, *refs):
    refs = list(refs)
    blocks = [refs.pop(0) for _ in range(n)]
    weights = [[[refs.pop(0) for _ in range(4)] for _ in range(2)] for _ in range(n)]
    acc_in = None if first else refs.pop(0)
    out_refs = refs
    for pair in range(2):
        total = None if first else acc_in[:, pair * 256 : pair * 256 + 256]
        for k in range(n):
            for line in range(2):
                both = jnp.concatenate(
                    [weights[k][line][2 * pair][...], weights[k][line][2 * pair + 1][...]], axis=1
                )
                part = dot(blocks[k][:, line * 256 : line * 256 + 256], both)
                total = part if total is None else total + part
        if last:
            out_refs[2 * pair][...] = total[:, :128].astype(BF)
            out_refs[2 * pair + 1][...] = total[:, 128:].astype(BF)
        else:
            out_refs[0][:, pair * 256 : pair * 256 + 256] = total


def out_part(blocks, weights, index, state, last):
    n = len(blocks)
    rows = blocks[0].shape[0]
    first = state is None
    whole = lambda i, idx: (0, 0)
    in_specs = [pl.BlockSpec((rows, 512), whole) for _ in range(n)]
    operands = list(blocks)
    for k in range(n):
        for line in range(2):
            for w in weights:
                in_specs.append(
                    pl.BlockSpec((256, 128), lambda i, idx, at=2 * k + line: (idx[at], 0))
                )
                operands.append(w)
    if not first:
        in_specs.append(pl.BlockSpec((rows, 512), whole))
        operands.append(state)
    if last:
        out_specs = [pl.BlockSpec((rows, 128), whole)] * 4
        out_shape = [jax.ShapeDtypeStruct((rows, 128), BF)] * 4
    else:
        out_specs = pl.BlockSpec((rows, 512), whole)
        out_shape = jax.ShapeDtypeStruct((rows, 512), F32)
    return pl.pallas_call(
        functools.partial(out_kernel, n, first, last),
        grid_spec=pltpu.PrefetchScalarGridSpec(
            num_scalar_prefetch=1, grid=(1,), in_specs=in_specs, out_specs=out_specs
        ),
        out_shape=out_shape,
        compiler_params=pltpu.CompilerParams(vmem_limit_bytes=24 * MB),
        cost_estimate=pl.CostEstimate(
            flops=2 * n * rows * 512 * 512, bytes_accessed=n * 655360, transcendentals=0
        ),
    )(index, *operands)


def ring(blocks, size):
    up_pairs = [(i, (i + 1) % size) for i in range(size)]
    down_pairs = [(i, (i - 1) % size) for i in range(size)]
    up = list(blocks)
    down = list(blocks)
    steps = [[(0, b) for b in blocks]]
    for d in range(1, size // 2):
        up = [lax.ppermute(b, "z", up_pairs) for b in up]
        down = [lax.ppermute(b, "z", down_pairs) for b in down]
        steps.append([(-d, b) for b in up] + [(d, b) for b in down])
    half = blocks[0].shape[0] // 2
    top = [lax.ppermute(b[:half], "z", up_pairs) for b in up]
    low = [lax.ppermute(b[half:], "z", down_pairs) for b in down]
    steps.append([(size // 2, jnp.concatenate([t, b], axis=0)) for t, b in zip(top, low)])
    return steps


def shards(
    tokens,
    sign_bits,
    norm_gain,
    code_indices,
    codebook,
    col_scale,
    group_ids,
    filters,
    skip_gain,
    out_weight,
):
    width = code_indices.shape[0]
    rows = tokens.shape[0]
    half = rows // 2
    depth = lax.axis_size("z")
    line = lax.axis_index("xl")
    z = lax.axis_index("z")
    core = lax.axis_index("core")
    seqs = lax.axis_size("seq")

    kept = lax.dynamic_slice_in_dim(tokens, core * half, half, 0)
    given = lax.dynamic_slice_in_dim(tokens, (1 - core) * half, half, 0)
    taken = lax.ppermute(given, "core", SWAP)
    block = jnp.where(
        core == 0,
        jnp.concatenate([kept, taken], axis=1),
        jnp.concatenate([taken, kept], axis=1),
    )
    across = lax.ppermute(block, "xl", SWAP)
    steps = ring([block, across], depth)

    signed = (2 * sign_bits - 1).astype(F32)
    row_scale = norm_gain * signed * (1.0 / float(np.sqrt(width)))
    row_scale = jnp.broadcast_to(row_scale[:, None], (width, 128))
    codes = jnp.transpose(code_indices, (1, 0, 2))
    had = jnp.asarray(hadamard_np(256), BF)
    scale3 = col_scale.reshape(3, 1, 128)
    weights = []
    for branch in range(3):
        own = make_weights(codebook, codes, scale3, row_scale, had, branch)
        weights.append((own, lax.ppermute(own, "core", SWAP)))

    picks = (group_ids[None, :] == jnp.arange(filters.shape[0], dtype=jnp.int32)[:, None]).astype(F32)
    taps = lax.dot_general(
        filters, picks, (((0,), (0,)), ((), ())), precision=lax.Precision.HIGHEST
    )
    flen = taps.shape[0]
    with_skip = jnp.concatenate([taps, jnp.broadcast_to(skip_gain[None, :], (8, 128))], axis=0)
    other = lax.ppermute(with_skip, "core", SWAP)
    taps_pair = (taps, other[:flen])
    skip_pair = (skip_gain.reshape(1, 128), other[flen : flen + 1])

    out_x = lax.ppermute(out_weight, "xl", SWAP)
    out_c = lax.ppermute(out_weight, "core", SWAP)
    out_d = lax.ppermute(out_x, "core", SWAP)
    out_ws = (out_weight, out_c, out_x, out_d)

    def feature_block(which, shift):
        return (line if which == 0 else 1 - line) * depth + (z + shift + depth) % depth

    state = None
    groups = [sum(steps[:3], []), steps[3], steps[4]]
    for g, group in enumerate(groups):
        order = []
        for pos, (shift, b) in enumerate(group):
            order.append(feature_block(pos % 2, shift))
        index = jnp.stack(order).astype(jnp.int32)
        state = project([b for _, b in group], weights, index, state, g == len(groups) - 1)
    gate, product = state

    rim = product[half - flen :]
    rim = jnp.concatenate([rim[:, 128:], rim[:, :128]], axis=1)
    count = 2 * seqs
    rim = lax.ppermute(rim, ("seq", "core"), [(i, i + 1) for i in range(count - 1)])
    flag = core.astype(jnp.int32).reshape(1)
    later = filtered_part(flag, product, 1, product, gate, 1, taps_pair, skip_pair)
    early = filtered_part(flag, rim, 0, product, gate, 0, taps_pair, skip_pair)

    outs = []
    for hidden in (later, early):
        mine = lax.dynamic_slice_in_dim(hidden, line * 128, 128, 0)
        theirs = lax.dynamic_slice_in_dim(hidden, (1 - line) * 128, 128, 0)
        came = lax.ppermute(theirs, "xl", SWAP)
        steps = ring([jnp.concatenate([mine, came], axis=1)], depth)
        state = None
        groups = [sum(steps[:3], []), sum(steps[3:], [])]
        for g, group in enumerate(groups):
            order = []
            for shift, b in group:
                order.append(feature_block(0, shift))
                order.append(feature_block(1, shift))
            index = jnp.stack(order).astype(jnp.int32)
            state = out_part([b for _, b in group], out_ws, index, state, g == len(groups) - 1)
        outs.append(state)
    later_out, early_out = outs

    pieces = [jnp.concatenate([e, l], axis=0) for e, l in zip(early_out, later_out)]
    own = pieces[0]
    from_core = lax.ppermute(pieces[1], "core", SWAP)
    from_x = lax.ppermute(pieces[2], "xl", SWAP)
    from_both = lax.ppermute(pieces[3], ("xl", "core"), [(0, 3), (1, 2), (2, 1), (3, 0)])

    def along_line(a, b):
        a = a.reshape(2, 1, 128, 128)
        b = b.reshape(2, 1, 128, 128)
        return jnp.where(
            line == 0, jnp.concatenate([a, b], axis=1), jnp.concatenate([b, a], axis=1)
        ).reshape(half, 128)

    same = along_line(own, from_x)
    diff = along_line(from_core, from_both)
    return jnp.where(
        core == 0, jnp.concatenate([same, diff], axis=0), jnp.concatenate([diff, same], axis=0)
    )


def solution(mesh):
    seqs = mesh.shape["seq"]
    depth = mesh.shape["ch"] // 4
    fine = Mesh(mesh.devices.reshape(seqs, 2, depth, 2), ("seq", "xl", "z", "core"))
    ch = ("xl", "z", "core")
    placed = (
        P("seq", ch),
        P(),
        P(),
        P(None, None, ch),
        P(),
        P(None, ch),
        P(ch),
        P(),
        P(ch),
        P(None, ch),
    )
    return jax.shard_map(
        shards, mesh=fine, in_specs=placed, out_specs=P("seq", ch), check_vma=False
    )
```

```python
import functools

import jax
import jax.numpy as jnp
import numpy as np
from jax import lax
from jax.experimental import pallas as pl
from jax.experimental.pallas import tpu as pltpu
from jax.sharding import Mesh
from jax.sharding import PartitionSpec as P

BF = jnp.bfloat16
F32 = jnp.float32
MB = 1024 * 1024
SWAP = [(0, 1), (1, 0)]


def hadamard_np(order):
    index = np.arange(order)
    anded = index[:, None] & index[None, :]
    parity = np.zeros((order, order), np.int64)
    for bit in range(order.bit_length()):
        parity += anded >> bit & 1
    return (1 - 2 * (parity % 2)).astype(np.float32)


def dot(a, b):
    return jnp.dot(a, b, preferred_element_type=F32)


def weight_kernel(book_ref, codes_ref, scale_ref, gain_ref, sign_ref, had_ref, out_ref, y_ref, rows_ref):
    outer = y_ref.shape[0]
    inner = y_ref.shape[1]
    branch = pl.program_id(0)

    @pl.when(branch == 0)
    def _():
        signed = (2 * sign_ref[...] - 1).astype(F32)
        scaled = gain_ref[...] * signed * (1.0 / float(np.sqrt(outer * inner)))
        for k in range(outer * inner // 128):
            spread = jnp.broadcast_to(scaled[k : k + 1, :], (128, 128))
            rows_ref[pl.ds(k * 128, 128), :] = spread.T

    scale = scale_ref[pl.ds(branch, 1), :]
    values = [(book_ref[k] * scale).astype(BF).astype(F32) for k in range(4)]
    had = had_ref[...]
    for a in range(outer):
        codes = codes_ref[0, pl.ds(a * inner, inner), :]
        low = jnp.where(codes == 0, values[0], values[1])
        high = jnp.where(codes == 2, values[2], values[3])
        levels = jnp.where(codes < 2, low, high).astype(BF)
        y_ref[a] = dot(had, levels)

    def mix(i, carry):
        at = pl.multiple_of(i * 16, 16)
        parts = [y_ref[a, pl.ds(at, 16), :] for a in range(outer)]
        span = 1
        while span < outer:
            new = list(parts)
            for a in range(outer):
                if a & span:
                    new[a] = parts[a ^ span] - parts[a]
                else:
                    new[a] = parts[a] + parts[a ^ span]
            parts = new
            span *= 2
        for a in range(outer):
            rows = pl.ds(a * inner + at, 16)
            out_ref[0, rows, :] = (parts[a] * rows_ref[rows, :]).astype(BF)
        return carry

    lax.fori_loop(0, inner // 16, mix, 0)


def make_weights(book, codes, scale, gain, sign, had):
    width = codes.shape[1]
    inner = had.shape[0]
    lines = width // 128
    return pl.pallas_call(
        weight_kernel,
        grid=(3,),
        in_specs=[
            pl.BlockSpec(memory_space=pltpu.SMEM),
            pl.BlockSpec((1, width, 128), lambda i: (i, 0, 0)),
            pl.BlockSpec((3, 128), lambda i: (0, 0)),
            pl.BlockSpec((lines, 128), lambda i: (0, 0)),
            pl.BlockSpec((lines, 128), lambda i: (0, 0)),
            pl.BlockSpec((inner, inner), lambda i: (0, 0)),
        ],
        out_specs=pl.BlockSpec((1, width, 128), lambda i: (i, 0, 0)),
        out_shape=jax.ShapeDtypeStruct((3, width, 128), BF),
        scratch_shapes=[
            pltpu.VMEM((width // inner, inner, 128), F32),
            pltpu.VMEM((width, 128), F32),
        ],
        compiler_params=pltpu.CompilerParams(vmem_limit_bytes=60 * MB),
        cost_estimate=pl.CostEstimate(
            flops=6 * width * inner * 128, bytes_accessed=width * 128 * 20, transcendentals=0
        ),
    )(book, codes, scale, gain.reshape(lines, 128), sign.reshape(lines, 128), had)


def project_kernel(n, first, last, width, idx_ref, *refs):
    refs = list(refs)
    blocks = [refs.pop(0) for _ in range(n)]
    weights = [refs.pop(0) for _ in range(2)]
    if not first:
        acc_in = refs.pop(0)
        sq_in = refs.pop(0)
    out_refs = refs[:2]
    w_buf, w_sems, x_buf, x_sems = refs[2:]
    moves = []
    for k in range(n):
        mine = [pltpu.make_async_copy(blocks[k], x_buf.at[k], x_sems.at[k])]
        rows = pl.ds(pl.multiple_of(idx_ref[k] * 256, 256), 256)
        for side in range(2):
            mine.append(
                pltpu.make_async_copy(
                    weights[side].at[:, rows],
                    w_buf.at[k, :, :, pl.ds(side * 128, 128)],
                    w_sems.at[k, side],
                )
            )
        for move in mine:
            move.start()
        moves.append(mine)
    squares = None if first else sq_in[...]
    totals = [None if first else acc_in[:, b * 256 : (b + 1) * 256] for b in range(3)]
    for k in range(n):
        for move in moves[k]:
            move.wait()
        block = x_buf[k]
        wide = block.astype(F32)
        wide = wide * wide
        part = wide[:, :128] + wide[:, 128:]
        squares = part if squares is None else squares + part
        for b in range(3):
            part = dot(block, w_buf[k, b])
            totals[b] = part if totals[b] is None else totals[b] + part
    if last:
        mean = jnp.sum(squares, axis=1, keepdims=True) / width
        inverse = lax.rsqrt(mean + 1e-05)
        out_refs[0][...] = totals[0] * inverse
        out_refs[1][...] = ((totals[1] * inverse) * (totals[2] * inverse)).astype(BF)
    else:
        for b in range(3):
            out_refs[0][:, b * 256 : (b + 1) * 256] = totals[b]
        out_refs[1][...] = squares


def project(blocks, weights, index, state, last):
    n = len(blocks)
    rows = blocks[0].shape[0]
    width = weights[0].shape[1]
    first = state is None
    far = pl.BlockSpec(memory_space=pltpu.HBM)
    near = pl.BlockSpec((rows, 256), lambda i, idx: (0, 0))
    in_specs = [far] * (n + 2)
    operands = list(blocks) + list(weights)
    wide_spec = pl.BlockSpec((rows, 768), lambda i, idx: (0, 0))
    sq_spec = pl.BlockSpec((rows, 128), lambda i, idx: (0, 0))
    if not first:
        in_specs += [wide_spec, sq_spec]
        operands += list(state)
    if last:
        out_specs = [near] * 2
        out_shape = [
            jax.ShapeDtypeStruct((rows, 256), F32),
            jax.ShapeDtypeStruct((rows, 256), BF),
        ]
    else:
        out_specs = [wide_spec, sq_spec]
        out_shape = [
            jax.ShapeDtypeStruct((rows, 768), F32),
            jax.ShapeDtypeStruct((rows, 128), F32),
        ]
    return pl.pallas_call(
        functools.partial(project_kernel, n, first, last, width),
        grid_spec=pltpu.PrefetchScalarGridSpec(
            num_scalar_prefetch=1,
            grid=(1,),
            in_specs=in_specs,
            out_specs=out_specs,
            scratch_shapes=[
                pltpu.VMEM((n, 3, 256, 256), BF),
                pltpu.SemaphoreType.DMA((n, 2)),
                pltpu.VMEM((n, rows, 256), BF),
                pltpu.SemaphoreType.DMA((n,)),
            ],
        ),
        out_shape=out_shape,
        compiler_params=pltpu.CompilerParams(vmem_limit_bytes=60 * MB),
        cost_estimate=pl.CostEstimate(
            flops=2 * n * rows * 256 * 768, bytes_accessed=n * 655360 + 3 * MB, transcendentals=0
        ),
    )(index, *operands)


def filter_kernel(flag_ref, prev_ref, cur_ref, gate_ref, taps_a, taps_b, skip_a, skip_b, give_ref, keep_ref, s_ref):
    lead = prev_ref.shape[0]
    ext = jnp.concatenate([prev_ref[...], cur_ref[...]], axis=0).astype(F32)
    s_ref[0] = ext
    for r in range(1, 8):
        s_ref[r] = pltpu.roll(ext, r, 0)
    here = flag_ref[0] == 0
    line = flag_ref[1]

    for out_ref, part in ((give_ref, 1 - line), (keep_ref, line)):
        at = pl.multiple_of(part * 128, 128)
        made = []
        for side, (taps, skip) in enumerate(((taps_a, skip_a), (taps_b, skip_b))):
            lanes = slice(side * 128, side * 128 + 128)
            total = jnp.zeros((128, 128), F32)
            for r in range(8):
                for q in range(lead // 8):
                    j = 8 * q + r
                    moved = s_ref[r, pl.ds(pl.multiple_of(at + lead - 8 * q, 8), 128), lanes]
                    total = total + taps[j : j + 1, :] * moved
            own = s_ref[0, pl.ds(pl.multiple_of(at + lead, 8), 128), lanes]
            total = total + skip[...] * own
            made.append(gate_ref[pl.ds(at, 128), lanes] * total)
        out_ref[:, 0:128] = jnp.where(here, made[0], made[1]).astype(BF)
        out_ref[:, 128:256] = jnp.where(here, made[1], made[0]).astype(BF)


def filtered_part(flag, prev, prev_at, product, gate, part, taps, skips):
    lead = taps[0].shape[0]
    whole = lambda i, flag: (0, 0)
    return pl.pallas_call(
        filter_kernel,
        grid_spec=pltpu.PrefetchScalarGridSpec(
            num_scalar_prefetch=1,
            grid=(1,),
            in_specs=[
                pl.BlockSpec((lead, 256), lambda i, flag: (prev_at, 0)),
                pl.BlockSpec((256, 256), lambda i, flag: (part, 0)),
                pl.BlockSpec((256, 256), lambda i, flag: (part, 0)),
                pl.BlockSpec((lead, 128), whole),
                pl.BlockSpec((lead, 128), whole),
                pl.BlockSpec((1, 128), whole),
                pl.BlockSpec((1, 128), whole),
            ],
            out_specs=[pl.BlockSpec((128, 256), whole)] * 2,
            scratch_shapes=[pltpu.VMEM((8, lead + 256, 256), F32)],
        ),
        out_shape=[jax.ShapeDtypeStruct((128, 256), BF)] * 2,
        compiler_params=pltpu.CompilerParams(vmem_limit_bytes=8 * MB),
        cost_estimate=pl.CostEstimate(
            flops=2 * 128 * 256 * 256 * 32, bytes_accessed=MB, transcendentals=0
        ),
    )(flag, prev, product, gate, taps[0], taps[1], skips[0], skips[1])


def out_kernel(n, first, last, idx_ref, *refs):
    refs = list(refs)
    blocks = [[refs.pop(0) for _ in range(2)] for _ in range(n)]
    weights = [[[refs.pop(0) for _ in range(4)] for _ in range(2)] for _ in range(n)]
    acc_in = None if first else refs.pop(0)
    out_refs = refs
    stacked = [jnp.concatenate([e[...], l[...]], axis=0) for e, l in blocks]
    for pair in range(2):
        total = None if first else acc_in[:, pair * 256 : pair * 256 + 256]
        for k in range(n):
            for line in range(2):
                both = jnp.concatenate(
                    [weights[k][line][2 * pair][...], weights[k][line][2 * pair + 1][...]], axis=1
                )
                part = dot(stacked[k][:, line * 256 : line * 256 + 256], both)
                total = part if total is None else total + part
        if last:
            out_refs[2 * pair][...] = total[:, :128].astype(BF)
            out_refs[2 * pair + 1][...] = total[:, 128:].astype(BF)
        else:
            out_refs[0][:, pair * 256 : pair * 256 + 256] = total


def out_part(blocks, weights, index, state, last):
    n = len(blocks)
    rows = 256
    first = state is None
    whole = lambda i, idx: (0, 0)
    in_specs = [pl.BlockSpec((128, 512), whole) for _ in range(2 * n)]
    operands = [b for pair in blocks for b in pair]
    for k in range(n):
        for line in range(2):
            for w in weights:
                in_specs.append(
                    pl.BlockSpec((256, 128), lambda i, idx, at=2 * k + line: (idx[at], 0))
                )
                operands.append(w)
    if not first:
        in_specs.append(pl.BlockSpec((rows, 512), whole))
        operands.append(state)
    if last:
        out_specs = [pl.BlockSpec((rows, 128), whole)] * 4
        out_shape = [jax.ShapeDtypeStruct((rows, 128), BF)] * 4
    else:
        out_specs = pl.BlockSpec((rows, 512), whole)
        out_shape = jax.ShapeDtypeStruct((rows, 512), F32)
    return pl.pallas_call(
        functools.partial(out_kernel, n, first, last),
        grid_spec=pltpu.PrefetchScalarGridSpec(
            num_scalar_prefetch=1, grid=(1,), in_specs=in_specs, out_specs=out_specs
        ),
        out_shape=out_shape,
        compiler_params=pltpu.CompilerParams(vmem_limit_bytes=12 * MB),
        cost_estimate=pl.CostEstimate(
            flops=2 * n * rows * 512 * 512, bytes_accessed=n * 655360, transcendentals=0
        ),
    )(index, *operands)


def tie(*values):
    return lax.optimization_barrier(values)


def shards(
    tokens,
    sign_bits,
    norm_gain,
    code_indices,
    codebook,
    col_scale,
    group_ids,
    filters,
    skip_gain,
    out_weight,
):
    width = code_indices.shape[0]
    rows = tokens.shape[0]
    half = rows // 2
    depth = lax.axis_size("z")
    line = lax.axis_index("xl")
    z = lax.axis_index("z")
    core = lax.axis_index("core")
    seqs = lax.axis_size("seq")

    up_pairs = [(i, (i + 1) % depth) for i in range(depth)]
    down_pairs = [(i, (i - 1) % depth) for i in range(depth)]

    def up(b):
        return lax.ppermute(b, "z", up_pairs)

    def down(b):
        return lax.ppermute(b, "z", down_pairs)

    def feature_block(which, shift):
        return (line if which == 0 else 1 - line) * depth + (z + shift + depth) % depth

    def indices(pairs):
        return jnp.stack([feature_block(w, s) for w, s in pairs]).astype(jnp.int32)

    kept = lax.dynamic_slice_in_dim(tokens, core * half, half, 0)
    given = lax.dynamic_slice_in_dim(tokens, (1 - core) * half, half, 0)
    taken = lax.ppermute(given, "core", SWAP)
    own0 = jnp.where(
        core == 0,
        jnp.concatenate([kept, taken], axis=1),
        jnp.concatenate([taken, kept], axis=1),
    )

    codes = jnp.transpose(code_indices, (1, 0, 2))
    had = jnp.asarray(hadamard_np(256), BF)

    last = depth // 2
    own_u1, own_d1 = up(own0), down(own0)
    near0 = lax.ppermute(own0, "xl", SWAP)
    w_own = make_weights(codebook, codes, col_scale, norm_gain, sign_bits, had)

    own_u1, own_d1, near0, w_own = tie(own_u1, own_d1, near0, w_own)
    own_u2, own_d2 = up(own_u1), down(own_d1)
    near_u1, near_d1 = up(near0), down(near0)
    w_other = lax.ppermute(w_own, "core", SWAP)

    own_u2, own_d2, out_weight, filters = tie(own_u2, own_d2, out_weight, filters)
    own_u3, own_d3 = up(own_u2), down(own_d2)
    out_x = lax.ppermute(out_weight, "xl", SWAP)
    picks = (group_ids[None, :] == jnp.arange(filters.shape[0], dtype=jnp.int32)[:, None]).astype(F32)
    taps = lax.dot_general(
        filters, picks, (((0,), (0,)), ((), ())), precision=lax.Precision.HIGHEST
    )
    flen = taps.shape[0]
    with_skip = jnp.concatenate([taps, jnp.broadcast_to(skip_gain[None, :], (8, 128))], axis=0)

    near_u1, near_d1, with_skip = tie(near_u1, near_d1, with_skip)
    near_u2, near_d2 = up(near_u1), down(near_d1)
    other = lax.ppermute(with_skip, "core", SWAP)
    taps_pair = (taps, other[:flen])
    skip_pair = (skip_gain.reshape(1, 128), other[flen : flen + 1])

    own_u3, own_d3, w_other = tie(own_u3, own_d3, w_other)
    own_4 = up(own_u3)
    weights = (w_own, w_other)
    state = project(
        [own0, near0, own_u1, own_d1, own_u2, own_d2, near_u1, near_d1],
        weights,
        indices([(0, 0), (1, 0), (0, -1), (0, 1), (0, -2), (0, 2), (1, -1), (1, 1)]),
        None,
        False,
    )

    near_u2, near_d2, out_x, out_weight = tie(near_u2, near_d2, out_x, out_weight)
    near_u3, near_d3 = up(near_u2), down(near_d2)
    out_c = lax.ppermute(out_weight, "core", SWAP)

    near_u3, near_d3, own_4, state = tie(near_u3, near_d3, own_4, state)
    near_4 = down(near_d3)
    out_d = lax.ppermute(out_x, "core", SWAP)
    out_ws = (out_weight, out_c, out_x, out_d)
    state = project(
        [near_u2, near_d2, own_u3, own_d3, own_4, near_u3, near_d3],
        weights,
        indices([(1, -2), (1, 2), (0, -3), (0, 3), (0, last), (1, -3), (1, 3)]),
        state,
        False,
    )

    near_4, state = tie(near_4, state)
    gate, product = project([near_4], weights, indices([(1, last)]), state, True)

    rim = product[half - flen :]
    rim = jnp.concatenate([rim[:, 128:], rim[:, :128]], axis=1)
    count = 2 * seqs
    rim = lax.ppermute(rim, ("seq", "core"), [(i, i + 1) for i in range(count - 1)])
    flag = jnp.stack([core, line]).astype(jnp.int32)

    def both(shifts):
        return indices([(w, s) for s in shifts for w in (0, 1)])

    give, keep = filtered_part(flag, product, 1, product, gate, 1, taps_pair, skip_pair)
    came = lax.ppermute(give, "xl", SWAP)
    rim, came = tie(rim, came)
    late0 = jnp.concatenate([keep, came], axis=1)
    give, keep = filtered_part(flag, rim, 0, product, gate, 0, taps_pair, skip_pair)
    late_u1, late_d1 = up(late0), down(late0)
    early0 = jnp.concatenate([keep, lax.ppermute(give, "xl", SWAP)], axis=1)
    early_u1, early_d1 = up(early0), down(early0)

    late_u1, late_d1, early0 = tie(late_u1, late_d1, early0)
    late_u2, late_d2 = up(late_u1), down(late_d1)

    early_u1, early_d1 = tie(early_u1, early_d1)
    early_u2, early_d2 = up(early_u1), down(early_d1)
    total = out_part(
        [(early0, late0), (early_u1, late_u1), (early_d1, late_d1)], out_ws, both((0, -1, 1)), None, False
    )

    late_u2, late_d2, total = tie(late_u2, late_d2, total)
    late_u3, late_d3 = up(late_u2), down(late_d2)

    early_u2, early_d2 = tie(early_u2, early_d2)
    early_u3, early_d3 = up(early_u2), down(early_d2)
    total = out_part([(early_u2, late_u2), (early_d2, late_d2)], out_ws, both((-2, 2)), total, False)

    late_u3, late_d3, total = tie(late_u3, late_d3, total)
    late_4 = up(late_u3)

    early_u3, early_d3 = tie(early_u3, early_d3)
    early_4 = down(early_d3)
    total = out_part([(early_u3, late_u3), (early_d3, late_d3)], out_ws, both((-3, 3)), total, False)
    early_4, late_4, total = tie(early_4, late_4, total)
    pieces = out_part([(early_4, late_4)], out_ws, both((last,)), total, True)

    own = pieces[0]
    from_core = lax.ppermute(pieces[1], "core", SWAP)
    from_x = lax.ppermute(pieces[2], "xl", SWAP)
    from_both = lax.ppermute(pieces[3], ("xl", "core"), [(0, 3), (1, 2), (2, 1), (3, 0)])

    def along_line(a, b):
        a = a.reshape(2, 1, 128, 128)
        b = b.reshape(2, 1, 128, 128)
        return jnp.where(
            line == 0, jnp.concatenate([a, b], axis=1), jnp.concatenate([b, a], axis=1)
        ).reshape(half, 128)

    same = along_line(own, from_x)
    diff = along_line(from_core, from_both)
    return jnp.where(
        core == 0, jnp.concatenate([same, diff], axis=0), jnp.concatenate([diff, same], axis=0)
    )


def solution(mesh):
    seqs = mesh.shape["seq"]
    depth = mesh.shape["ch"] // 4
    fine = Mesh(mesh.devices.reshape(seqs, 2, depth, 2), ("seq", "xl", "z", "core"))
    ch = ("xl", "z", "core")
    placed = (
        P("seq", ch),
        P(),
        P(),
        P(None, None, ch),
        P(),
        P(None, ch),
        P(ch),
        P(),
        P(ch),
        P(None, ch),
    )
    return jax.shard_map(
        shards, mesh=fine, in_specs=placed, out_specs=P("seq", ch), check_vma=False
    )
```

```python
import functools

import jax
import jax.numpy as jnp
import numpy as np
from jax import lax
from jax.experimental import pallas as pl
from jax.experimental.pallas import tpu as pltpu
from jax.sharding import Mesh
from jax.sharding import PartitionSpec as P

BF = jnp.bfloat16
F32 = jnp.float32
MB = 1024 * 1024
SWAP = [(0, 1), (1, 0)]


def hadamard_np(order):
    index = np.arange(order)
    anded = index[:, None] & index[None, :]
    parity = np.zeros((order, order), np.int64)
    for bit in range(order.bit_length()):
        parity += anded >> bit & 1
    return (1 - 2 * (parity % 2)).astype(np.float32)


def dot(a, b):
    return jnp.dot(a, b, preferred_element_type=F32)


def weight_kernel(book_ref, codes_ref, scale_ref, gain_ref, sign_ref, had_ref, out_ref, y_ref, rows_ref):
    outer = y_ref.shape[0]
    inner = y_ref.shape[1]
    branch = pl.program_id(0)

    @pl.when(branch == 0)
    def _():
        signed = (2 * sign_ref[...] - 1).astype(F32)
        scaled = gain_ref[...] * signed * (1.0 / float(np.sqrt(outer * inner)))
        for k in range(outer * inner // 128):
            spread = jnp.broadcast_to(scaled[k : k + 1, :], (128, 128))
            rows_ref[pl.ds(k * 128, 128), :] = spread.T

    scale = scale_ref[pl.ds(branch, 1), :]
    values = [(book_ref[k] * scale).astype(BF).astype(F32) for k in range(4)]
    had = had_ref[...]
    for a in range(outer):
        codes = codes_ref[0, pl.ds(a * inner, inner), :]
        low = jnp.where(codes == 0, values[0], values[1])
        high = jnp.where(codes == 2, values[2], values[3])
        levels = jnp.where(codes < 2, low, high).astype(BF)
        y_ref[a] = dot(had, levels)

    def mix(i, carry):
        at = pl.multiple_of(i * 16, 16)
        parts = [y_ref[a, pl.ds(at, 16), :] for a in range(outer)]
        span = 1
        while span < outer:
            new = list(parts)
            for a in range(outer):
                if a & span:
                    new[a] = parts[a ^ span] - parts[a]
                else:
                    new[a] = parts[a] + parts[a ^ span]
            parts = new
            span *= 2
        for a in range(outer):
            rows = pl.ds(a * inner + at, 16)
            out_ref[0, rows, :] = (parts[a] * rows_ref[rows, :]).astype(BF)
        return carry

    lax.fori_loop(0, inner // 16, mix, 0)


def make_weights(book, codes, scale, gain, sign, had):
    width = codes.shape[1]
    inner = had.shape[0]
    lines = width // 128
    return pl.pallas_call(
        weight_kernel,
        grid=(3,),
        in_specs=[
            pl.BlockSpec(memory_space=pltpu.SMEM),
            pl.BlockSpec((1, width, 128), lambda i: (i, 0, 0)),
            pl.BlockSpec((3, 128), lambda i: (0, 0)),
            pl.BlockSpec((lines, 128), lambda i: (0, 0)),
            pl.BlockSpec((lines, 128), lambda i: (0, 0)),
            pl.BlockSpec((inner, inner), lambda i: (0, 0)),
        ],
        out_specs=pl.BlockSpec((1, width, 128), lambda i: (i, 0, 0)),
        out_shape=jax.ShapeDtypeStruct((3, width, 128), BF),
        scratch_shapes=[
            pltpu.VMEM((width // inner, inner, 128), F32),
            pltpu.VMEM((width, 128), F32),
        ],
        compiler_params=pltpu.CompilerParams(vmem_limit_bytes=60 * MB),
        cost_estimate=pl.CostEstimate(
            flops=6 * width * inner * 128, bytes_accessed=width * 128 * 20, transcendentals=0
        ),
    )(book, codes, scale, gain.reshape(lines, 128), sign.reshape(lines, 128), had)


def project_kernel(sources, count, spots, first, last, width, idx_ref, *refs):
    refs = list(refs)
    arrays = [refs.pop(0) for _ in range(count)]
    n = len(sources)
    weights = [refs.pop(0) for _ in range(2)]
    if not first:
        acc_in = refs.pop(0)
        sq_in = refs.pop(0)
    outs = 3 if last else 2
    out_refs = refs[:outs]
    w_buf, w_sems, x_buf, x_sems = refs[outs:]
    moves = []
    for k in range(n):
        mine = []
        size = x_buf.shape[1] // len(sources[k])
        for piece, (number, start) in enumerate(sources[k]):
            mine.append(
                pltpu.make_async_copy(
                    arrays[number].at[pl.ds(start, size)],
                    x_buf.at[k, pl.ds(piece * size, size)],
                    x_sems.at[k, piece],
                )
            )
        rows = pl.ds(pl.multiple_of(idx_ref[spots[k]] * 256, 256), 256)
        for side in range(2):
            mine.append(
                pltpu.make_async_copy(
                    weights[side].at[:, rows],
                    w_buf.at[k, :, :, pl.ds(side * 128, 128)],
                    w_sems.at[k, side],
                )
            )
        for move in mine:
            move.start()
        moves.append(mine)
    squares = None if first else sq_in[...]
    totals = [None if first else acc_in[:, b * 256 : (b + 1) * 256] for b in range(3)]
    for k in range(n):
        for move in moves[k]:
            move.wait()
        block = x_buf[k]
        wide = block.astype(F32)
        wide = wide * wide
        part = wide[:, :128] + wide[:, 128:]
        squares = part if squares is None else squares + part
        for b in range(3):
            part = dot(block, w_buf[k, b])
            totals[b] = part if totals[b] is None else totals[b] + part
    if last:
        mean = jnp.sum(squares, axis=1, keepdims=True) / width
        inverse = lax.rsqrt(mean + 1e-05)
        out_refs[0][...] = totals[0] * inverse
        product = ((totals[1] * inverse) * (totals[2] * inverse)).astype(BF)
        out_refs[1][...] = product
        rim = product[product.shape[0] - 128 :]
        out_refs[2][:, :128] = rim[:, 128:]
        out_refs[2][:, 128:] = rim[:, :128]
    else:
        for b in range(3):
            out_refs[0][:, b * 256 : (b + 1) * 256] = totals[b]
        out_refs[1][...] = squares


def project(rows, arrays, sources, weights, table, index, state, last):
    n = len(sources)
    width = weights[0].shape[1]
    first = state is None
    far = pl.BlockSpec(memory_space=pltpu.HBM)
    near = pl.BlockSpec((rows, 256), lambda i, idx: (0, 0))
    in_specs = [far] * (len(arrays) + 2)
    operands = list(arrays) + list(weights)
    wide_spec = pl.BlockSpec((rows, 768), lambda i, idx: (0, 0))
    sq_spec = pl.BlockSpec((rows, 128), lambda i, idx: (0, 0))
    if not first:
        in_specs += [wide_spec, sq_spec]
        operands += list(state)
    if last:
        out_specs = [near] * 2 + [pl.BlockSpec((128, 256), lambda i, idx: (0, 0))]
        out_shape = [
            jax.ShapeDtypeStruct((rows, 256), F32),
            jax.ShapeDtypeStruct((rows, 256), BF),
            jax.ShapeDtypeStruct((128, 256), BF),
        ]
    else:
        out_specs = [wide_spec, sq_spec]
        out_shape = [
            jax.ShapeDtypeStruct((rows, 768), F32),
            jax.ShapeDtypeStruct((rows, 128), F32),
        ]
    return pl.pallas_call(
        functools.partial(project_kernel, sources, len(arrays), index, first, last, width),
        grid_spec=pltpu.PrefetchScalarGridSpec(
            num_scalar_prefetch=1,
            grid=(1,),
            in_specs=in_specs,
            out_specs=out_specs,
            scratch_shapes=[
                pltpu.VMEM((n, 3, 256, 256), BF),
                pltpu.SemaphoreType.DMA((n, 2)),
                pltpu.VMEM((n, rows, 256), BF),
                pltpu.SemaphoreType.DMA((n, 2)),
            ],
        ),
        out_shape=out_shape,
        compiler_params=pltpu.CompilerParams(vmem_limit_bytes=(58 if last else 60) * MB),
        cost_estimate=pl.CostEstimate(
            flops=2 * n * rows * 256 * 768, bytes_accessed=n * 655360 + 3 * MB, transcendentals=0
        ),
    )(table, *operands)


def filter_kernel(flag_ref, prev_ref, cur_ref, gate_ref, taps_a, taps_b, skip_a, skip_b, give_ref, keep_ref, s_ref):
    lead = prev_ref.shape[0]
    ext = jnp.concatenate([prev_ref[...], cur_ref[...]], axis=0).astype(F32)
    s_ref[0] = ext
    for r in range(1, 8):
        s_ref[r] = pltpu.roll(ext, r, 0)
    size = flag_ref.shape[0]
    here = flag_ref[size - 2] == 0
    line = flag_ref[size - 1]

    for out_ref, part in ((give_ref, 1 - line), (keep_ref, line)):
        at = pl.multiple_of(part * 128, 128)
        made = []
        for side, (taps, skip) in enumerate(((taps_a, skip_a), (taps_b, skip_b))):
            lanes = slice(side * 128, side * 128 + 128)
            total = jnp.zeros((128, 128), F32)
            for r in range(8):
                for q in range(lead // 8):
                    j = 8 * q + r
                    moved = s_ref[r, pl.ds(pl.multiple_of(at + lead - 8 * q, 8), 128), lanes]
                    total = total + taps[j : j + 1, :] * moved
            own = s_ref[0, pl.ds(pl.multiple_of(at + lead, 8), 128), lanes]
            total = total + skip[...] * own
            made.append(gate_ref[pl.ds(at, 128), lanes] * total)
        out_ref[:, 0:128] = jnp.where(here, made[0], made[1]).astype(BF)
        out_ref[:, 128:256] = jnp.where(here, made[1], made[0]).astype(BF)


def filtered_part(flag, prev, prev_at, product, gate, part, taps, skips):
    lead = taps[0].shape[0]
    whole = lambda i, flag: (0, 0)
    return pl.pallas_call(
        filter_kernel,
        grid_spec=pltpu.PrefetchScalarGridSpec(
            num_scalar_prefetch=1,
            grid=(1,),
            in_specs=[
                pl.BlockSpec((lead, 256), lambda i, flag: (prev_at, 0)),
                pl.BlockSpec((256, 256), lambda i, flag: (part, 0)),
                pl.BlockSpec((256, 256), lambda i, flag: (part, 0)),
                pl.BlockSpec((lead, 128), whole),
                pl.BlockSpec((lead, 128), whole),
                pl.BlockSpec((1, 128), whole),
                pl.BlockSpec((1, 128), whole),
            ],
            out_specs=[pl.BlockSpec((128, 256), whole)] * 2,
            scratch_shapes=[pltpu.VMEM((8, lead + 256, 256), F32)],
        ),
        out_shape=[jax.ShapeDtypeStruct((128, 256), BF)] * 2,
        compiler_params=pltpu.CompilerParams(vmem_limit_bytes=8 * MB),
        cost_estimate=pl.CostEstimate(
            flops=2 * 128 * 256 * 256 * 32, bytes_accessed=MB, transcendentals=0
        ),
    )(flag, prev, product, gate, taps[0], taps[1], skips[0], skips[1])


def out_kernel(n, first, last, *refs):
    refs = list(refs)[1:]
    blocks = [[refs.pop(0) for _ in range(2)] for _ in range(n)]
    weights = [[[refs.pop(0) for _ in range(4)] for _ in range(2)] for _ in range(n)]
    acc_in = None if first else refs.pop(0)
    out_refs = refs
    stacked = [jnp.concatenate([e[...], l[...]], axis=0) for e, l in blocks]
    for pair in range(2):
        total = None if first else acc_in[:, pair * 256 : pair * 256 + 256]
        for k in range(n):
            for line in range(2):
                both = jnp.concatenate(
                    [weights[k][line][2 * pair][...], weights[k][line][2 * pair + 1][...]], axis=1
                )
                part = dot(stacked[k][:, line * 256 : line * 256 + 256], both)
                total = part if total is None else total + part
        if last:
            out_refs[2 * pair][...] = total[:, :128].astype(BF)
            out_refs[2 * pair + 1][...] = total[:, 128:].astype(BF)
        else:
            out_refs[0][:, pair * 256 : pair * 256 + 256] = total


def out_part(blocks, weights, table, index, state, last):
    n = len(blocks)
    rows = 256
    first = state is None
    whole = lambda i, idx: (0, 0)
    in_specs = [pl.BlockSpec((128, 512), whole) for _ in range(2 * n)]
    operands = [b for pair in blocks for b in pair]
    for k in range(n):
        for line in range(2):
            for w in weights:
                in_specs.append(
                    pl.BlockSpec((256, 128), lambda i, idx, at=index[2 * k + line]: (idx[at], 0))
                )
                operands.append(w)
    if not first:
        in_specs.append(pl.BlockSpec((rows, 512), whole))
        operands.append(state)
    if last:
        out_specs = [pl.BlockSpec((rows, 128), whole)] * 4
        out_shape = [jax.ShapeDtypeStruct((rows, 128), BF)] * 4
    else:
        out_specs = pl.BlockSpec((rows, 512), whole)
        out_shape = jax.ShapeDtypeStruct((rows, 512), F32)
    return pl.pallas_call(
        functools.partial(out_kernel, n, first, last),
        grid_spec=pltpu.PrefetchScalarGridSpec(
            num_scalar_prefetch=1, grid=(1,), in_specs=in_specs, out_specs=out_specs
        ),
        out_shape=out_shape,
        compiler_params=pltpu.CompilerParams(vmem_limit_bytes=12 * MB),
        cost_estimate=pl.CostEstimate(
            flops=2 * n * rows * 512 * 512, bytes_accessed=n * 655360, transcendentals=0
        ),
    )(table, *operands)


def tie(*values):
    return lax.optimization_barrier(values)


def shards(
    tokens,
    sign_bits,
    norm_gain,
    code_indices,
    codebook,
    col_scale,
    group_ids,
    filters,
    skip_gain,
    out_weight,
):
    width = code_indices.shape[0]
    rows = tokens.shape[0]
    half = rows // 2
    depth = lax.axis_size("z")
    line = lax.axis_index("xl")
    z = lax.axis_index("z")
    core = lax.axis_index("core")
    seqs = lax.axis_size("seq")

    up_pairs = [(i, (i + 1) % depth) for i in range(depth)]
    down_pairs = [(i, (i - 1) % depth) for i in range(depth)]

    def up(b):
        return lax.ppermute(b, "z", up_pairs)

    def down(b):
        return lax.ppermute(b, "z", down_pairs)

    def feature_block(which, shift):
        return (line if which == 0 else 1 - line) * depth + (z + shift + depth) % depth

    half_turn = depth // 2
    places = [(w, s) for w in (0, 1) for s in range(1 - half_turn, half_turn + 1)]
    table = jnp.stack([feature_block(w, s) for w, s in places] + [core, line]).astype(jnp.int32)

    def indices(pairs):
        return [places.index(pair) for pair in pairs]

    kept = lax.dynamic_slice_in_dim(tokens, core * half, half, 0)
    given = lax.dynamic_slice_in_dim(tokens, (1 - core) * half, half, 0)
    taken = lax.ppermute(given, "core", SWAP)
    own0 = jnp.where(
        core == 0,
        jnp.concatenate([kept, taken], axis=1),
        jnp.concatenate([taken, kept], axis=1),
    )

    codes = jnp.transpose(code_indices, (1, 0, 2))
    had = jnp.asarray(hadamard_np(256), BF)

    last = depth // 2
    own_u1, own_d1 = up(own0), down(own0)
    near0 = lax.ppermute(own0, "xl", SWAP)
    picks = (group_ids[None, :] == jnp.arange(filters.shape[0], dtype=jnp.int32)[:, None]).astype(F32)
    taps = lax.dot_general(
        filters, picks, (((0,), (0,)), ((), ())), precision=lax.Precision.HIGHEST
    )
    flen = taps.shape[0]
    with_skip = jnp.concatenate([taps, jnp.broadcast_to(skip_gain[None, :], (8, 128))], axis=0)
    other = lax.ppermute(with_skip, "core", SWAP)
    taps_pair = (taps, other[:flen])
    skip_pair = (skip_gain.reshape(1, 128), other[flen : flen + 1])

    own_u1, own_d1, near0, codes, other, table = tie(own_u1, own_d1, near0, codes, other, table)
    both_u, both_d = jnp.concatenate([own_u1, near0], axis=0), jnp.concatenate([own_d1, near0], axis=0)
    two_u, two_d = up(both_u), down(both_d)
    w_own = make_weights(codebook, codes, col_scale, norm_gain, sign_bits, had)

    two_u, two_d, w_own, out_weight = tie(two_u, two_d, w_own, out_weight)
    three_u, three_d = up(two_u), down(two_d)
    w_other = lax.ppermute(w_own, "core", SWAP)
    out_x = lax.ppermute(out_weight, "xl", SWAP)
    weights = (w_own, w_other)

    three_u, three_d, out_weight = tie(three_u, three_d, out_weight)
    out_c = lax.ppermute(out_weight, "core", SWAP)
    four_u, four_d = up(three_u), down(three_d)
    far_row = half
    state = project(
        half,
        [own0, both_u, both_d, two_u, two_d, three_u, three_d],
        [
            [(0, 0)],
            [(1, 0)],
            [(1, far_row)],
            [(2, 0)],
            [(3, 0)],
            [(3, far_row)],
            [(4, 0)],
            [(4, far_row)],
            [(5, 0)],
            [(5, far_row)],
            [(6, 0)],
            [(6, far_row)],
        ],
        weights,
        table,
        indices(
            [(0, 0), (0, -1), (1, 0), (0, 1)]
            + [(0, -2), (1, -1), (0, 2), (1, 1), (0, -3), (1, -2), (0, 3), (1, 2)]
        ),
        None,
        False,
    )

    four_u, four_d, state, out_x, out_c = tie(four_u, four_d, state, out_x, out_c)
    cut = half // 2
    near_4u, near_4d = up(four_u[half : half + cut]), down(four_d[half + cut :])
    out_d = lax.ppermute(out_x, "core", SWAP)
    out_ws = (out_weight, out_c, out_x, out_d)
    gate, product, rim = project(
        half,
        [four_u, four_d, near_4u, near_4d],
        [[(0, 0)], [(0, far_row)], [(1, far_row)], [(2, 0), (3, 0)]],
        weights,
        table,
        indices([(0, last), (1, -3), (1, 3), (1, last)]),
        state,
        True,
    )

    count = 2 * seqs
    rim = lax.ppermute(rim, ("seq", "core"), [(i, i + 1) for i in range(count - 1)])
    flag = table

    def both(shifts):
        return indices([(w, s) for s in shifts for w in (0, 1)])

    give, keep = filtered_part(flag, product, 1, product, gate, 1, taps_pair, skip_pair)
    came = lax.ppermute(give, "xl", SWAP)
    rim, came, out_d = tie(rim, came, out_d)
    out_ws = (out_weight, out_c, out_x, out_d)
    late0 = jnp.concatenate([keep, came], axis=1)
    give, keep = filtered_part(flag, rim, 0, product, gate, 0, taps_pair, skip_pair)
    late_u1, late_d1 = up(late0), down(late0)
    early0 = jnp.concatenate([keep, lax.ppermute(give, "xl", SWAP)], axis=1)
    early_u1, early_d1 = up(early0), down(early0)

    late_u1, late_d1, early0 = tie(late_u1, late_d1, early0)
    late_u2, late_d2 = up(late_u1), down(late_d1)

    early_u1, early_d1 = tie(early_u1, early_d1)
    early_u2, early_d2 = up(early_u1), down(early_d1)
    total = out_part(
        [(early0, late0), (early_u1, late_u1), (early_d1, late_d1)], out_ws, table, both((0, -1, 1)), None, False
    )

    late_u2, late_d2, total = tie(late_u2, late_d2, total)
    late_u3, late_d3 = up(late_u2), down(late_d2)

    early_u2, early_d2 = tie(early_u2, early_d2)
    early_u3, early_d3 = up(early_u2), down(early_d2)
    total = out_part([(early_u2, late_u2), (early_d2, late_d2)], out_ws, table, both((-2, 2)), total, False)

    late_u3, late_d3, total = tie(late_u3, late_d3, total)
    late_4 = up(late_u3)

    early_u3, early_d3 = tie(early_u3, early_d3)
    early_4 = down(early_d3)
    total = out_part([(early_u3, late_u3), (early_d3, late_d3)], out_ws, table, both((-3, 3)), total, False)
    early_4, late_4, total = tie(early_4, late_4, total)
    pieces = out_part([(early_4, late_4)], out_ws, table, both((last,)), total, True)

    own = pieces[0]
    from_core = lax.ppermute(pieces[1], "core", SWAP)
    from_x = lax.ppermute(pieces[2], "xl", SWAP)
    from_both = lax.ppermute(pieces[3], ("xl", "core"), [(0, 3), (1, 2), (2, 1), (3, 0)])

    def along_line(a, b):
        a = a.reshape(2, 1, 128, 128)
        b = b.reshape(2, 1, 128, 128)
        return jnp.where(
            line == 0, jnp.concatenate([a, b], axis=1), jnp.concatenate([b, a], axis=1)
        ).reshape(half, 128)

    same = along_line(own, from_x)
    diff = along_line(from_core, from_both)
    return jnp.where(
        core == 0, jnp.concatenate([same, diff], axis=0), jnp.concatenate([diff, same], axis=0)
    )


def solution(mesh):
    seqs = mesh.shape["seq"]
    depth = mesh.shape["ch"] // 4
    fine = Mesh(mesh.devices.reshape(seqs, 2, depth, 2), ("seq", "xl", "z", "core"))
    ch = ("xl", "z", "core")
    placed = (
        P("seq", ch),
        P(),
        P(),
        P(None, None, ch),
        P(),
        P(None, ch),
        P(ch),
        P(),
        P(ch),
        P(None, ch),
    )
    return jax.shard_map(
        shards, mesh=fine, in_specs=placed, out_specs=P("seq", ch), check_vma=False
    )
```
